512 devices in a mesh: tile: 32 (over y, x, core), member: 16 (over z).
Axes of the slice: x: 4, y: 4, z: 16, core: 2. Of those that a mesh axis runs over, the one named last changes fastest.
Arguments:
- hx: bfloat16 [512, 131072], P('member', 'tile'), may hold values from -6 to 6
- obs_value: bfloat16 [131072], P('tile'), may hold values from -8 to 8
- obs_rinv: bfloat16 [131072], P('tile'), may hold values from 0.29882812 to 4
- obs_index: int32 [512, 1024], P('tile'), may hold values from 128 to 6015, as said below
- loc_weight: float32 [512, 1024], P(('tile', 'member')), may hold values from 0.05 to 1
- state: bfloat16 [512, 524288], P('member', 'tile'), may hold values from -6 to 6
Outputs:
- analysis: bfloat16 [512, 524288], P('member', 'tile')
The draws below stay inside these ranges and needn't reach their ends.
Inputs may be any that keep to these rules, and one draw needn't show every extreme that they name: `obs_index`: row p lists 1024 distinct positions in the pool of tile p // 16: positions 0 .. 1023 are the last 1024 observations of the tile before it, the next 4096 the tile's own, the last 1024 the first observations of the tile after it; the tiles form a closed band. All positions of a row lie within 2048 consecutive positions.
All inputs are finite; a program needn't handle non-finite values.
Results may differ from the reference program's by a relative error of at most 0.012.
The reference program's roundings to bfloat16 on the way (of `obs_block`, `scaled`, `transform` and `state_pert`) count: a program that leaves them out, or rounds other values in their place, can miss the bound.
Values may be sent and summed in bfloat16 or wider, within the bound.
A program may use at most 64 MiB of HBM per device.

```python
import math
import jax
import jax.numpy as jnp
from jax import lax

ENS = 512
NOBS_DEV = 4096
LOC = 1024
CELLS_DEV = 16384
NS_ITERS = 3
NOBS = 131072
CELLS = 524288
PATCHES = 512
N_MEMBER = 16


def draw_obs_index(key, part):
    patch_pos = jnp.arange(PATCHES, dtype=jnp.int32) % N_MEMBER
    starts = (2 * patch_pos + 1) * NOBS_DEV // (2 * N_MEMBER)
    keys = jax.random.split(key, PATCHES)
    offsets = jax.vmap(lambda single: jax.random.permutation(single, 2 * LOC)[:LOC])(keys)
    return (starts[:, None] + offsets).astype(jnp.int32)


def shard_levels(rng, extent, cuts, smallest, top_value):
    loudness, own = 1.0, jax.random.fold_in(rng, 6)
    for dim, blocks in cuts:
        heights = jnp.exp(jax.random.uniform(jax.random.fold_in(own, dim), (blocks,), jnp.float32, smallest / len(cuts), top_value / len(cuts)))
        loudness = loudness * jnp.repeat(heights, extent[dim] // blocks).reshape([-1 if axis == dim else 1 for axis in range(len(extent))])
    return loudness


def noise(key, shape, deviation, most, cuts=(), kind=jnp.bfloat16):
    result = deviation * jax.random.normal(key, shape, jnp.float32)
    if cuts:
        result = result * shard_levels(key, shape, cuts, -0.22, 0.18)
    return jnp.clip(result, -most, most).astype(kind)


def setup_inputs(seed: int = 0) -> dict:
    splits = jax.random.split(jax.random.key(seed), 7)
    hx = noise(splits[0], (ENS, NOBS), 1.0, 6.0, ((0, 16), (1, 32)))
    obs_value = noise(splits[1], (NOBS,), 1.5, 8.0, ((0, 32),))
    obs_rinv = jnp.clip(jnp.exp(math.log(4.0) - 2.594181 * jax.random.uniform(splits[2], (NOBS,), jnp.float32) ** shard_levels(splits[2], (NOBS,), ((0, 32),), -0.2, 0.2)), 0.29882812, 4.0).astype(jnp.bfloat16)
    obs_index = draw_obs_index(jax.random.fold_in(splits[6], 71), 0)
    loc_weight = jnp.clip(jnp.exp(math.log(1.0) - 2.9957323 * jax.random.uniform(splits[4], (PATCHES, LOC), jnp.float32) ** shard_levels(splits[4], (PATCHES, LOC), ((0, 512),), -0.2, 0.2)), 0.05, 1.0)
    state = noise(splits[5], (ENS, CELLS), 1.0, 6.0, ((0, 16), (1, 32)))
    return {"hx": hx, "obs_value": obs_value, "obs_rinv": obs_rinv, "obs_index": obs_index, "loc_weight": loc_weight, "state": state}


def product_f32(left, right, dims):
    return lax.dot_general(left.astype(jnp.float32), right.astype(jnp.float32), (dims, ((), ())), precision=lax.Precision.HIGHEST, preferred_element_type=jnp.float32)

def analysis(obs_block, obs_pair, loc_row):
    members = obs_block.shape[0]
    block_f = obs_block.astype(jnp.float32)
    obs_mean = lax.optimization_barrier(jnp.mean(block_f, axis=0))
    obs_root = jnp.sqrt(obs_pair[1].astype(jnp.float32) * loc_row)
    scaled = ((block_f - obs_mean) * obs_root).astype(jnp.bfloat16)
    innovation = (obs_pair[0].astype(jnp.float32) - obs_mean) * obs_root
    gram_matrix = product_f32(scaled, scaled, ((1,), (1,)))
    identity = jnp.eye(members, dtype=jnp.float32)
    system = gram_matrix + (members - 1.0) * identity
    projection = jnp.dot(scaled.astype(jnp.float32), innovation, precision=lax.Precision.HIGHEST)
    norm_a = jnp.sqrt(jnp.sum(system * system))
    upper_iter = system / norm_a
    lower_iter = identity
    for sweep in range(NS_ITERS):
        upper_b = upper_iter.astype(jnp.bfloat16)
        lower_b = lower_iter.astype(jnp.bfloat16)
        product = product_f32(lower_b, upper_b, ((1,), (0,)))
        half_step = (1.5 * identity - 0.5 * product).astype(jnp.bfloat16)
        if sweep + 1 < NS_ITERS:
            upper_iter = product_f32(upper_b, half_step, ((1,), (0,)))
        lower_iter = product_f32(half_step, lower_b, ((1,), (0,)))
    invroot = lower_iter / jnp.sqrt(norm_a)
    inner_w = jnp.dot(invroot, projection, precision=lax.Precision.HIGHEST)
    mean_w = jnp.dot(invroot, inner_w, precision=lax.Precision.HIGHEST)
    transform = jnp.sqrt(members - 1.0) * invroot + mean_w[:, None]
    return transform.astype(jnp.bfloat16)

def transform_state(transform, state_block):
    block_f = state_block.astype(jnp.float32)
    state_mean = lax.optimization_barrier(jnp.mean(block_f, axis=0))
    state_pert = (block_f - state_mean).astype(jnp.bfloat16)
    combined = product_f32(transform, state_pert, ((0,), (0,)))
    return (state_mean + combined).astype(jnp.bfloat16)

def reference(hx, obs_value, obs_rinv, obs_index, loc_weight, state):
    obs_total = hx.shape[1]
    patch_cells = CELLS_DEV // N_MEMBER

    def one_patch(patch):
        tile_pos = patch // N_MEMBER
        index_row = lax.dynamic_index_in_dim(obs_index, patch, 0, keepdims=False)
        global_cols = ((tile_pos * NOBS_DEV - LOC + index_row) % obs_total).astype(jnp.int32)
        obs_block = jnp.take(hx, global_cols, axis=1)
        obs_pair = jnp.stack([jnp.take(obs_value, global_cols), jnp.take(obs_rinv, global_cols)])
        loc_row = lax.dynamic_index_in_dim(loc_weight, patch, 0, keepdims=False)
        transform = analysis(obs_block, obs_pair, loc_row)
        start = (patch * patch_cells).astype(jnp.int32)
        state_block = lax.dynamic_slice_in_dim(state, start, patch_cells, 1)
        return transform_state(transform, state_block)
    blocks = lax.map(one_patch, jnp.arange(PATCHES, dtype=jnp.int32))
    return jnp.transpose(blocks, (1, 0, 2)).reshape(ENS, PATCHES * patch_cells)
```

```python
import functools

import jax
import jax.numpy as jnp
from jax import lax
from jax.experimental import pallas as pl
from jax.experimental.pallas import tpu as pltpu
from jax.sharding import PartitionSpec as P

MESH = pl.DeviceIdType.MESH
F32, BF16 = jnp.float32, jnp.bfloat16
LOC = 1024
NS_ITERS = 3
LANES = 128
ROWS = 128
CHUNKS = 2


def mm(left, right, dims=((1,), (0,)), precision=None):
    return lax.dot_general(
        left, right, (dims, ((), ())), precision=precision, preferred_element_type=F32
    )


def kernel(
    n, tiles,
    hx_ref, pair_ref, index_ref, weight_ref, state_ref,
    out_ref,
    pool, pair_pool, halo, pair_halo, stage, obs, recv, scaled, system, upper, lower, half,
    trans, pert, result,
    halo_send, halo_recv, obs_send, obs_recv, in_send, in_recv, back_send, back_recv, own_sem,
):
    me = lax.axis_index("member")
    tile = lax.axis_index("tile")
    nxt, prv = lax.rem(tile + 1, tiles), lax.rem(tile + tiles - 1, tiles)
    rows = hx_ref.shape[0]
    own = hx_ref.shape[1]
    members = rows * n
    width = LOC // CHUNKS

    def peer(d):
        return lax.rem(me + d, n)

    def nth(k):
        step = n // 2 - (k + 1) // 2
        return jnp.where(k % 2 == 1, step, n - step)

    barrier = pltpu.get_barrier_semaphore()
    for d in range(1, n):
        pl.semaphore_signal(barrier, inc=1, device_id={"member": peer(d)}, device_id_type=MESH)
    for other in (nxt, prv):
        pl.semaphore_signal(barrier, inc=1, device_id={"tile": other}, device_id_type=MESH)

    pool[:, pl.ds(LOC, own)] = hx_ref[...].astype(F32)
    pair_pool[0:2, pl.ds(LOC, own)] = pair_ref[...]

    pl.semaphore_wait(barrier, n + 1)

    def halo_copies():
        copies = []
        for slot, (other, start) in enumerate(((nxt, own - LOC), (prv, 0))):
            for src, dst, place in (
                (hx_ref.at[:, pl.ds(start, LOC)], halo.at[slot], slot),
                (pair_ref.at[:, pl.ds(start, LOC)], pair_halo.at[slot], 2 + slot),
            ):
                copies.append(pltpu.make_async_remote_copy(
                    src_ref=src, dst_ref=dst, send_sem=halo_send.at[place],
                    recv_sem=halo_recv.at[place], device_id={"tile": other}, device_id_type=MESH,
                ))
        return copies

    def in_copy(d, c):
        t = peer(d)
        return pltpu.make_async_remote_copy(
            src_ref=state_ref.at[:, pl.ds(pl.multiple_of(t * LOC + c * width, LANES), width)],
            dst_ref=recv.at[pl.ds(pl.multiple_of(me * rows, rows), rows), pl.ds(c * width, width)],
            send_sem=in_send.at[c, d], recv_sem=in_recv.at[c, d],
            device_id={"member": t}, device_id_type=MESH,
        )

    def obs_copy(d):
        return pltpu.make_async_remote_copy(
            src_ref=stage.at[d],
            dst_ref=obs.at[pl.ds(pl.multiple_of(me * rows, rows), rows), :],
            send_sem=obs_send.at[d], recv_sem=obs_recv.at[d],
            device_id={"member": peer(d)}, device_id_type=MESH,
        )

    def back_copy(d, c):
        t = peer(d)
        return pltpu.make_async_remote_copy(
            src_ref=result.at[pl.ds(pl.multiple_of(t * rows, rows), rows), pl.ds(c * width, width)],
            dst_ref=out_ref.at[:, pl.ds(pl.multiple_of(me * LOC + c * width, LANES), width)],
            send_sem=back_send.at[c, d], recv_sem=back_recv.at[c, d],
            device_id={"member": t}, device_id_type=MESH,
        )

    halos = halo_copies()
    for copy in halos:
        copy.start()

    def start_in(c):
        def body(k, carry):
            in_copy(nth(k), c).start()
            return carry
        lax.fori_loop(0, n - 1, body, 0)

    start_in(0)
    own_state = pltpu.make_async_copy(
        state_ref.at[:, pl.ds(pl.multiple_of(me * LOC, LOC), LOC)],
        recv.at[pl.ds(pl.multiple_of(me * rows, rows), rows), :], own_sem.at[0],
    )
    own_state.start()

    for copy in halos:
        copy.wait()
    for slot, place in ((0, 0), (1, LOC + own)):
        pool[:, pl.ds(place, LOC)] = halo[slot].astype(F32)
        pair_pool[0:2, pl.ds(place, LOC)] = pair_halo[slot]

    def gather(source, height, patch, put):
        row = index_ref[pl.ds(patch, 1), :]
        group, lane = row >> 7, row & (LANES - 1)
        for g in range(LOC // LANES):
            cut = slice(g * LANES, (g + 1) * LANES)
            lane_b = jnp.broadcast_to(lane[:, cut], (height, LANES))
            group_b = jnp.broadcast_to(group[:, cut], (height, LANES))
            value = jnp.zeros((height, LANES), F32)
            for h in range(source.shape[1] // LANES):
                found = jnp.take_along_axis(
                    source[:, h * LANES:(h + 1) * LANES], lane_b, axis=1)
                value = jnp.where(group_b == h, found, value)
            put(cut, value)

    def gather_for(k, carry):
        d = nth(k)

        def put(cut, value):
            stage[d, :, cut] = value.astype(BF16)

        gather(pool, rows, peer(d), put)
        obs_copy(d).start()
        return carry

    lax.fori_loop(0, n - 1, gather_for, 0)
    for c in range(1, CHUNKS):
        start_in(c)

    def put_own(cut, value):
        obs[pl.ds(pl.multiple_of(me * rows, rows), rows), cut] = value.astype(BF16)

    gather(pool, rows, me, put_own)
    sel = []
    gather(pair_pool, pair_pool.shape[0], me, lambda cut, value: sel.append(value))
    value_row = jnp.concatenate([part[0:1] for part in sel], axis=1)
    rinv_row = jnp.concatenate([part[1:2] for part in sel], axis=1)
    root = jnp.sqrt(rinv_row * weight_ref[...])

    def wait_obs(d, carry):
        obs_copy(d).wait()
        return carry

    lax.fori_loop(1, n, wait_obs, 0)

    parts = []
    step = 256
    for s in range(0, LOC, step):
        cut = slice(s, s + step)
        block = obs[:, cut].astype(F32)
        mean = jnp.sum(block, axis=0, keepdims=True) * (1.0 / members)
        scaled[:, cut] = ((block - mean) * root[:, cut]).astype(BF16)
        parts.append((value_row[:, cut] - mean) * root[:, cut])
    innovation = jnp.concatenate(parts, axis=1)
    high = innovation.astype(BF16).astype(F32)
    mid = (innovation - high).astype(BF16).astype(F32)
    low = innovation - high - mid
    split = jnp.concatenate([high, mid, low, jnp.zeros((13, LOC), F32)], axis=0).astype(BF16)
    projection = jnp.sum(mm(split, scaled[...], ((1,), (1,))), axis=0, keepdims=True)

    def eye(r):
        shape = (ROWS, members)
        return (lax.broadcasted_iota(jnp.int32, shape, 0) + r
                == lax.broadcasted_iota(jnp.int32, shape, 1))

    pieces = range(0, members, ROWS)
    square = jnp.zeros((1, members), F32)
    for r in pieces:
        gram = mm(scaled[r:r + ROWS, :], scaled[...], ((1,), (1,)))
        piece = jnp.where(eye(r), gram + (members - 1.0), gram)
        system[r:r + ROWS, :] = piece
        square = square + jnp.sum(piece * piece, axis=0, keepdims=True)
    norm = jnp.sqrt(jnp.sum(square, axis=1, keepdims=True))

    def half_of(product, r):
        scaled_product = -0.5 * product
        return jnp.where(eye(r), 1.5 + scaled_product, scaled_product).astype(BF16)

    for r in pieces:
        first = (system[r:r + ROWS, :] / norm).astype(BF16)
        upper[0, r:r + ROWS, :] = first
        lower[0, r:r + ROWS, :] = half_of(first.astype(F32), r)
    for r in pieces:
        upper[1, r:r + ROWS, :] = mm(upper[0, r:r + ROWS, :], lower[0]).astype(BF16)
    for sweep in range(1, NS_ITERS):
        up, new_up = sweep % 2, (sweep + 1) % 2
        low_now, low_new = (sweep - 1) % 2, sweep % 2
        for r in pieces:
            half[r:r + ROWS, :] = half_of(mm(lower[low_now, r:r + ROWS, :], upper[up]), r)
        if sweep + 1 < NS_ITERS:
            for r in pieces:
                upper[new_up, r:r + ROWS, :] = mm(upper[up, r:r + ROWS, :], half[...]).astype(BF16)
            for r in pieces:
                lower[low_new, r:r + ROWS, :] = mm(half[r:r + ROWS, :], lower[low_now]).astype(BF16)
        else:
            for r in pieces:
                system[r:r + ROWS, :] = mm(half[r:r + ROWS, :], lower[low_now]) / jnp.sqrt(norm)
    invroot = system
    highest = lax.Precision.HIGHEST
    vector = jnp.broadcast_to(projection, (8, members))
    for _ in range(2):
        vector = mm(vector, invroot[...], ((1,), (1,)), highest)
    mean_w = vector[0:1]
    scale = (members - 1.0) ** 0.5
    for r in pieces:
        trans[r:r + ROWS, :] = (scale * invroot[:, r:r + ROWS].T + mean_w).astype(BF16)

    own_state.wait()
    own_back = []
    for c in range(CHUNKS):
        def wait_in(d, carry):
            in_copy(d, c).wait()
            return carry

        lax.fori_loop(1, n, wait_in, 0)
        cut = slice(c * width, (c + 1) * width)
        block = recv[:, cut].astype(F32)
        mean = jnp.sum(block, axis=0, keepdims=True) * (1.0 / members)
        pert[...] = (block - mean).astype(BF16)
        for r in pieces:
            result[r:r + ROWS, cut] = (mean + mm(trans[r:r + ROWS, :], pert[...])).astype(BF16)

        def start_back(k, carry):
            back_copy(nth(k), c).start()
            return carry

        lax.fori_loop(0, n - 1, start_back, 0)
        copy = pltpu.make_async_copy(
            result.at[pl.ds(pl.multiple_of(me * rows, rows), rows), pl.ds(c * width, width)],
            out_ref.at[:, pl.ds(pl.multiple_of(me * LOC + c * width, LANES), width)],
            own_sem.at[1 + c],
        )
        copy.start()
        own_back.append(copy)
    for c in range(CHUNKS):
        def wait_back(d, carry):
            back_copy(d, c).wait()
            return carry

        lax.fori_loop(1, n, wait_back, 0)
        own_back[c].wait()


def on_device(n, tiles, hx, obs_value, obs_rinv, obs_index, loc_weight, state):
    rows, own = hx.shape
    members = rows * n
    pair = jnp.stack([obs_value, obs_rinv]).astype(F32)
    vmem, anywhere = pl.BlockSpec(memory_space=pltpu.VMEM), pl.BlockSpec(memory_space=pl.ANY)
    dma = pltpu.SemaphoreType.DMA
    pool_width = own + 2 * LOC
    return pl.pallas_call(
        functools.partial(kernel, n, tiles),
        out_shape=jax.ShapeDtypeStruct(state.shape, BF16),
        in_specs=[vmem, vmem, vmem, vmem, anywhere],
        out_specs=anywhere,
        scratch_shapes=[
            pltpu.VMEM((rows, pool_width), F32),
            pltpu.VMEM((8, pool_width), F32),
            pltpu.VMEM((2, rows, LOC), BF16),
            pltpu.VMEM((2, 2, LOC), F32),
            pltpu.VMEM((n, rows, LOC), BF16),
            pltpu.VMEM((members, LOC), BF16),
            pltpu.VMEM((members, LOC), BF16),
            pltpu.VMEM((members, LOC), BF16),
            pltpu.VMEM((members, members), F32),
            pltpu.VMEM((2, members, members), BF16),
            pltpu.VMEM((2, members, members), BF16),
            pltpu.VMEM((members, members), BF16),
            pltpu.VMEM((members, members), BF16),
            pltpu.VMEM((members, LOC // CHUNKS), BF16),
            pltpu.VMEM((members, LOC), BF16),
            dma((4,)), dma((4,)), dma((n,)), dma((n,)),
            dma((CHUNKS, n)), dma((CHUNKS, n)), dma((CHUNKS, n)), dma((CHUNKS, n)),
            dma((1 + CHUNKS,)),
        ],
        compiler_params=pltpu.CompilerParams(
            collective_id=0, has_side_effects=True, vmem_limit_bytes=56 << 20
        ),
        cost_estimate=pl.CostEstimate(
            flops=3 * 10**9, bytes_accessed=4 * 2**20, transcendentals=0),
    )(hx, pair, obs_index, loc_weight, state)


def solution(mesh):
    in_specs = (
        P("member", "tile"),
        P("tile"),
        P("tile"),
        P("tile", None),
        P(("tile", "member"), None),
        P("member", "tile"),
    )
    return jax.shard_map(
        functools.partial(on_device, mesh.shape["member"], mesh.shape["tile"]),
        mesh=mesh, in_specs=in_specs, out_specs=P("member", "tile"), check_vma=False,
    )
```

```python
import functools

import jax
import jax.numpy as jnp
from jax import lax
from jax.experimental import pallas as pl
from jax.experimental.pallas import tpu as pltpu
from jax.sharding import PartitionSpec as P

MESH = pl.DeviceIdType.MESH
F32, BF16 = jnp.float32, jnp.bfloat16
LOC = 1024
NS_ITERS = 3
LANES = 128
ROWS = 128
WINDOW = 17
CHUNKS = 2
FILL = (
    ((0, 4), (0, 3)),
    ((0, 6),),
    ((0, 5),),
    ((0, 7),),
    ((0, 8), (0, 2), (0, 1), (1, 7), (1, 6)),
    ((1, 8), (1, 5), (1, 4), (1, 3), (1, 2), (1, 1)),
)
NEAR = 4
CUTS = 2


def mm(left, right, dims=((1,), (0,)), precision=None):
    return lax.dot_general(
        left, right, (dims, ((), ())), precision=precision, preferred_element_type=F32
    )


def kernel(
    n, tiles,
    hx_ref, pair_ref, index_hbm, weight_hbm, state_ref,
    out_ref,
    pool, wide, pair_pool, pair_wide, index_ref, weight_ref, picked, stage, obs, recv, scaled, system,
    upper, lower, half, trans, pert, result,
    hop_send, hop_recv, halo_send, halo_recv, pair_send, pair_recv, far_send, far_recv,
    in_send, in_recv, back_send, back_recv, own_sem, reach_sem,
):
    me = lax.axis_index("member")
    tile = lax.axis_index("tile")
    nxt, prv = lax.rem(tile + 1, tiles), lax.rem(tile + tiles - 1, tiles)
    rows, own = hx_ref.shape
    members = rows * n
    total = own + 2 * LOC
    width = LOC // CHUNKS
    cut_width = own // CUTS

    def peer(d):
        return lax.rem(me + d + n, n)

    def member_rows(m):
        return pl.ds(pl.multiple_of(m * rows, rows), rows)

    def nth(k):
        step = n // 2 - (k + 1) // 2
        return jnp.where(k % 2 == 1, step, n - step)

    def greet(semaphore, axis, others):
        for other in others:
            pl.semaphore_signal(semaphore, inc=1, device_id={axis: other}, device_id_type=MESH)

    barrier = pltpu.get_barrier_semaphore()
    greet(barrier, "member", (peer(1), peer(-1)))
    greet(barrier, "tile", (nxt, prv))
    local = [
        pltpu.make_async_copy(index_hbm, index_ref, own_sem.at[0]),
        pltpu.make_async_copy(weight_hbm, weight_ref, own_sem.at[1]),
        pltpu.make_async_copy(hx_ref, pool.at[0, :, pl.ds(LOC, own)], own_sem.at[2]),
        pltpu.make_async_copy(
            state_ref.at[:, pl.ds(pl.multiple_of(me * LOC, LOC), LOC)],
            recv.at[member_rows(me), :], own_sem.at[3]),
        pltpu.make_async_copy(pair_ref, pair_pool.at[:, pl.ds(LOC, own)], own_sem.at[4]),
    ]
    for copy in local:
        copy.start()
    pl.semaphore_wait(barrier, 4)

    def hop_copy(h, way, c):
        source = hx_ref if h == 1 else pool.at[2 * h - 3 + way]
        start = c * cut_width
        return pltpu.make_async_remote_copy(
            src_ref=source.at[:, pl.ds(start + (0 if h == 1 else LOC), cut_width)],
            dst_ref=pool.at[2 * h - 1 + way, :, pl.ds(LOC + start, cut_width)],
            send_sem=hop_send.at[h - 1, way, c], recv_sem=hop_recv.at[h - 1, way, c],
            device_id={"member": peer(1 - 2 * way)}, device_id_type=MESH,
        )

    def halo_copy(slot, side):
        source = hx_ref if slot == 0 else pool.at[slot]
        start = (0 if slot == 0 else LOC) + (0 if side else own - LOC)
        return pltpu.make_async_remote_copy(
            src_ref=source.at[:, pl.ds(start, LOC)],
            dst_ref=pool.at[slot, :, pl.ds(LOC + own if side else 0, LOC)],
            send_sem=halo_send.at[slot, side], recv_sem=halo_recv.at[slot, side],
            device_id={"tile": prv if side else nxt}, device_id_type=MESH,
        )

    def pair_copy(side):
        return pltpu.make_async_remote_copy(
            src_ref=pair_ref.at[:, pl.ds(0 if side else own - LOC, LOC)],
            dst_ref=pair_pool.at[:, pl.ds(LOC + own if side else 0, LOC)],
            send_sem=pair_send.at[side], recv_sem=pair_recv.at[side],
            device_id={"tile": prv if side else nxt}, device_id_type=MESH,
        )

    def far_copy(way, j):
        target = peer(j if way == 0 else -j)
        source_rows = member_rows(peer(-NEAR if way == 0 else NEAR))
        lanes = pl.ds(0, LOC)
        if j == n // 2 - NEAR:
            lanes = pl.ds(way * (LOC // 2), LOC // 2)
        return pltpu.make_async_remote_copy(
            src_ref=stage.at[way, j - 1, :, lanes],
            dst_ref=obs.at[source_rows, lanes],
            send_sem=far_send.at[way, j - 1], recv_sem=far_recv.at[way, j - 1],
            device_id={"member": target}, device_id_type=MESH,
        )

    def in_copy(d, c):
        t = peer(d)
        return pltpu.make_async_remote_copy(
            src_ref=state_ref.at[:, pl.ds(pl.multiple_of(t * LOC + c * width, LANES), width)],
            dst_ref=recv.at[member_rows(me), pl.ds(c * width, width)],
            send_sem=in_send.at[c, d], recv_sem=in_recv.at[c, d],
            device_id={"member": t}, device_id_type=MESH,
        )

    def back_copy(d, c):
        t = peer(d)
        return pltpu.make_async_remote_copy(
            src_ref=result.at[member_rows(t), pl.ds(c * width, width)],
            dst_ref=out_ref.at[:, pl.ds(pl.multiple_of(me * LOC + c * width, LANES), width)],
            send_sem=back_send.at[c, d], recv_sem=back_recv.at[c, d],
            device_id={"member": t}, device_id_type=MESH,
        )

    def fill(place):
        for c, d in FILL[place]:
            for distance in sorted({d, n - d}):
                in_copy(distance, c).start()

    for c in range(CUTS):
        for way in range(2):
            hop_copy(1, way, c).start()
    for side in range(2):
        pair_copy(side).start()
        halo_copy(0, side).start()

    known, stage_no = 1, 0
    while known < n // 2:
        greet(reach_sem.at[stage_no], "member", (peer(known), peer(-known)))
        pl.semaphore_wait(reach_sem.at[stage_no], 2)
        known, stage_no = (2 * known if stage_no else 2), stage_no + 1

    for copy in local:
        copy.wait()

    def pick(source, height, patch, puts):
        row = index_ref[pl.ds(patch, 1), :]
        last = total // LANES - WINDOW
        first = jnp.minimum(jnp.min(row, axis=1, keepdims=True) >> 7, last)
        offset = row - first * LANES
        group, lane = offset >> 7, offset & (LANES - 1)
        shape = (8, LANES)
        steps = [bit for bit in (32, 16, 8, 4, 2, 1) if bit <= last]
        chosen = [jnp.broadcast_to(first & bit, shape) != 0 for bit in steps]

        def body(r, carry):
            line = pl.ds(pl.multiple_of(r * 8, 8), 8)
            found = [source[line, h * LANES:(h + 1) * LANES] for h in range(total // LANES)]
            for bit, mask in zip(steps, chosen):
                found = [jnp.where(mask, found[i + bit], found[i])
                         for i in range(min(WINDOW + bit - 1, len(found) - bit))]
            for g in range(LOC // LANES):
                cut = slice(g * LANES, (g + 1) * LANES)
                lane_b = jnp.broadcast_to(lane[:, cut], shape)
                group_b = jnp.broadcast_to(group[:, cut], shape)
                value = jnp.take_along_axis(found[0], lane_b, axis=1)
                for h in range(1, WINDOW):
                    moved = jnp.take_along_axis(found[h], lane_b, axis=1)
                    value = jnp.where(group_b == h, moved, value)
                puts[line, cut] = value
            return carry

        lax.fori_loop(0, height // 8, body, 0)

    def widen(slot):
        wide[...] = pool[slot].astype(F32)

    def near_pick(slot, m):
        for side in range(2):
            halo_copy(slot, side).wait_recv()
        widen(slot)
        pick(wide, rows, me, picked)
        obs[member_rows(m), :] = picked[...].astype(BF16)

    fill(0)
    for h in range(1, NEAR + 1):
        for c in range(CUTS):
            for way in range(2):
                hop_copy(h, way, c).wait_recv()
                if h < NEAR:
                    hop_copy(h + 1, way, c).start()
        for way in range(2):
            for side in range(2):
                halo_copy(2 * h - 1 + way, side).start()
        fill(h)
        if h == 1:
            near_pick(0, me)
        if h > 1:
            for way in range(2):
                near_pick(2 * h - 3 + way, peer((h - 1) * (2 * way - 1)))
    for way in range(2):
        slot = 2 * NEAR - 1 + way
        for side in range(2):
            halo_copy(slot, side).wait_recv()
        widen(slot)
        for j in range(n // 2 - NEAR, 0, -1):
            pick(wide, rows, peer(j if way == 0 else -j), picked)
            stage[way, j - 1] = picked[...].astype(BF16)
            far_copy(way, j).start()
    fill(NEAR + 1)
    for way in range(2):
        widen(2 * NEAR - 1 + way)
        pick(wide, rows, me, picked)
        obs[member_rows(peer(NEAR * (2 * way - 1))), :] = picked[...].astype(BF16)

    for side in range(2):
        pair_copy(side).wait_recv()
    pair_wide[...] = jnp.zeros_like(pair_wide)
    pair_wide[0:2, :] = pair_pool[...]
    pick(pair_wide, 8, me, picked)
    value_row, rinv_row = picked[0:1, :], picked[1:2, :]
    root = jnp.sqrt(rinv_row * weight_ref[...])

    for way in range(2):
        for j in range(n // 2 - NEAR, 0, -1):
            far_copy(way, j).wait()

    parts = []
    step = 256
    for s in range(0, LOC, step):
        cut = slice(s, s + step)
        block = obs[:, cut].astype(F32)
        mean = jnp.sum(block, axis=0, keepdims=True) * (1.0 / members)
        scaled[:, cut] = ((block - mean) * root[:, cut]).astype(BF16)
        parts.append((value_row[:, cut] - mean) * root[:, cut])
    innovation = jnp.concatenate(parts, axis=1)
    high = innovation.astype(BF16).astype(F32)
    mid = (innovation - high).astype(BF16).astype(F32)
    low = innovation - high - mid
    split = jnp.concatenate([high, mid, low, jnp.zeros((13, LOC), F32)], axis=0).astype(BF16)
    projection = jnp.sum(mm(split, scaled[...], ((1,), (1,))), axis=0, keepdims=True)

    def eye(r):
        shape = (ROWS, members)
        return (lax.broadcasted_iota(jnp.int32, shape, 0) + r
                == lax.broadcasted_iota(jnp.int32, shape, 1))

    pieces = range(0, members, ROWS)
    square = jnp.zeros((1, members), F32)
    for r in pieces:
        gram = mm(scaled[r:r + ROWS, :], scaled[...], ((1,), (1,)))
        piece = jnp.where(eye(r), gram + (members - 1.0), gram)
        system[r:r + ROWS, :] = piece
        square = square + jnp.sum(piece * piece, axis=0, keepdims=True)
    norm = jnp.sqrt(jnp.sum(square, axis=1, keepdims=True))

    def half_of(product, r):
        scaled_product = -0.5 * product
        return jnp.where(eye(r), 1.5 + scaled_product, scaled_product).astype(BF16)

    for r in pieces:
        first = (system[r:r + ROWS, :] / norm).astype(BF16)
        upper[0, r:r + ROWS, :] = first
        lower[0, r:r + ROWS, :] = half_of(first.astype(F32), r)
    for r in pieces:
        upper[1, r:r + ROWS, :] = mm(upper[0, r:r + ROWS, :], lower[0]).astype(BF16)
    for sweep in range(1, NS_ITERS):
        up, new_up = sweep % 2, (sweep + 1) % 2
        low_now, low_new = (sweep - 1) % 2, sweep % 2
        for r in pieces:
            half[r:r + ROWS, :] = half_of(mm(lower[low_now, r:r + ROWS, :], upper[up]), r)
        if sweep + 1 < NS_ITERS:
            for r in pieces:
                upper[new_up, r:r + ROWS, :] = mm(upper[up, r:r + ROWS, :], half[...]).astype(BF16)
            for r in pieces:
                lower[low_new, r:r + ROWS, :] = mm(half[r:r + ROWS, :], lower[low_now]).astype(BF16)
        else:
            for r in pieces:
                system[r:r + ROWS, :] = mm(half[r:r + ROWS, :], lower[low_now]) / jnp.sqrt(norm)
    invroot = system
    highest = lax.Precision.HIGHEST
    vector = jnp.broadcast_to(projection, (8, members))
    for _ in range(2):
        vector = mm(vector, invroot[...], ((1,), (1,)), highest)
    mean_w = vector[0:1]
    scale = (members - 1.0) ** 0.5
    for r in pieces:
        trans[r:r + ROWS, :] = (scale * invroot[:, r:r + ROWS].T + mean_w).astype(BF16)

    own_back = []
    for c in range(CHUNKS):
        def wait_in(d, carry):
            in_copy(d, c).wait()
            return carry

        lax.fori_loop(1, n, wait_in, 0)
        cut = slice(c * width, (c + 1) * width)
        block = recv[:, cut].astype(F32)
        mean = jnp.sum(block, axis=0, keepdims=True) * (1.0 / members)
        pert[...] = (block - mean).astype(BF16)
        for r in pieces:
            result[r:r + ROWS, cut] = (mean + mm(trans[r:r + ROWS, :], pert[...])).astype(BF16)

        def start_back(k, carry):
            back_copy(nth(k), c).start()
            return carry

        lax.fori_loop(0, n - 1, start_back, 0)
        copy = pltpu.make_async_copy(
            result.at[member_rows(me), pl.ds(c * width, width)],
            out_ref.at[:, pl.ds(pl.multiple_of(me * LOC + c * width, LANES), width)],
            own_sem.at[5 + c],
        )
        copy.start()
        own_back.append(copy)
    for c in range(CHUNKS):
        def wait_back(d, carry):
            back_copy(d, c).wait()
            return carry

        lax.fori_loop(1, n, wait_back, 0)
        own_back[c].wait()
    for side in range(2):
        pair_copy(side).wait_send()
        for slot in range(2 * NEAR + 1):
            halo_copy(slot, side).wait_send()
    for h in range(1, NEAR + 1):
        for way in range(2):
            for c in range(CUTS):
                hop_copy(h, way, c).wait_send()


def on_device(n, tiles, hx, obs_value, obs_rinv, obs_index, loc_weight, state):
    rows, own = hx.shape
    members = rows * n
    pair = jnp.stack([obs_value, obs_rinv]).astype(F32)
    hbm = pl.BlockSpec(memory_space=pltpu.HBM)
    dma = pltpu.SemaphoreType.DMA
    total = own + 2 * LOC
    return pl.pallas_call(
        functools.partial(kernel, n, tiles),
        out_shape=jax.ShapeDtypeStruct(state.shape, BF16),
        in_specs=[hbm] * 5,
        out_specs=pl.BlockSpec(memory_space=pltpu.VMEM),
        scratch_shapes=[
            pltpu.VMEM((2 * NEAR + 1, rows, total), BF16),
            pltpu.VMEM((rows, total), F32),
            pltpu.VMEM((2, total), F32),
            pltpu.VMEM((8, total), F32),
            pltpu.VMEM((n, LOC), jnp.int32),
            pltpu.VMEM((1, LOC), F32),
            pltpu.VMEM((rows, LOC), F32),
            pltpu.VMEM((2, n // 2 - NEAR, rows, LOC), BF16),
            pltpu.VMEM((members, LOC), BF16),
            pltpu.VMEM((members, LOC), BF16),
            pltpu.VMEM((members, LOC), BF16),
            pltpu.VMEM((members, members), F32),
            pltpu.VMEM((2, members, members), BF16),
            pltpu.VMEM((2, members, members), BF16),
            pltpu.VMEM((members, members), BF16),
            pltpu.VMEM((members, members), BF16),
            pltpu.VMEM((members, LOC // CHUNKS), BF16),
            pltpu.VMEM((members, LOC), BF16),
            dma((NEAR, 2, CUTS)), dma((NEAR, 2, CUTS)),
            dma((2 * NEAR + 1, 2)), dma((2 * NEAR + 1, 2)), dma((2,)), dma((2,)),
            dma((2, n // 2 - NEAR)), dma((2, n // 2 - NEAR)),
            dma((CHUNKS, n)), dma((CHUNKS, n)), dma((CHUNKS, n)), dma((CHUNKS, n)),
            dma((5 + CHUNKS,)), pltpu.SemaphoreType.REGULAR((4,)),
        ],
        compiler_params=pltpu.CompilerParams(
            collective_id=0, has_side_effects=True, vmem_limit_bytes=40 << 20
        ),
        cost_estimate=pl.CostEstimate(
            flops=3 * 10**9, bytes_accessed=4 * 2**20, transcendentals=0),
    )(hx, pair, obs_index, loc_weight, state)


def solution(mesh):
    in_specs = (
        P("member", "tile"),
        P("tile"),
        P("tile"),
        P("tile", None),
        P(("tile", "member"), None),
        P("member", "tile"),
    )
    return jax.shard_map(
        functools.partial(on_device, mesh.shape["member"], mesh.shape["tile"]),
        mesh=mesh, in_specs=in_specs, out_specs=P("member", "tile"), check_vma=False,
    )
```

```python
import functools

import jax
import jax.numpy as jnp
from jax import lax
from jax.experimental import pallas as pl
from jax.experimental.pallas import tpu as pltpu
from jax.sharding import PartitionSpec as P

MESH = pl.DeviceIdType.MESH
F32, BF16 = jnp.float32, jnp.bfloat16
LOC = 1024
NS_ITERS = 3
LANES = 128
ROWS = 128
WINDOW = 17
CHUNKS = 2
FILL = (
    ((0, 4), (0, 3)),
    ((0, 6),),
    ((0, 5),),
    ((0, 7),),
    ((0, 8), (0, 2), (0, 1), (1, 7), (1, 6)),
    ((1, 8), (1, 5), (1, 4), (1, 3), (1, 2), (1, 1)),
)
NEAR = 4
CUTS = 2


def mm(left, right, dims=((1,), (0,)), precision=None):
    return lax.dot_general(
        left, right, (dims, ((), ())), precision=precision, preferred_element_type=F32
    )


def kernel(
    n, tiles,
    hx_ref, value_ref, rinv_ref, index_hbm, weight_hbm, state_ref,
    out_ref,
    pool, wide, pairs, pair_wide, index_ref, weight_ref, picked, stage, obs, recv, scaled, system,
    upper, lower, half, trans, pert, result,
    hop_send, hop_recv, halo_send, halo_recv, pair_send, pair_recv, far_send, far_recv,
    in_send, in_recv, back_send, back_recv, own_sem, reach_sem,
):
    me = lax.axis_index("member")
    tile = lax.axis_index("tile")
    nxt, prv = lax.rem(tile + 1, tiles), lax.rem(tile + tiles - 1, tiles)
    rows, own = hx_ref.shape
    members = rows * n
    total = own + 2 * LOC
    width = LOC // CHUNKS
    cut_width = own // CUTS

    def peer(d):
        return lax.rem(me + d + n, n)

    def member_rows(m):
        return pl.ds(pl.multiple_of(m * rows, rows), rows)

    def nth(k):
        step = n // 2 - (k + 1) // 2
        return jnp.where(k % 2 == 1, step, n - step)

    def greet(semaphore, axis, others):
        for other in others:
            pl.semaphore_signal(semaphore, inc=1, device_id={axis: other}, device_id_type=MESH)

    barrier = pltpu.get_barrier_semaphore()
    greet(barrier, "member", (peer(1), peer(-1)))
    greet(barrier, "tile", (nxt, prv))
    local = [
        pltpu.make_async_copy(index_hbm, index_ref, own_sem.at[0]),
        pltpu.make_async_copy(weight_hbm, weight_ref, own_sem.at[1]),
        pltpu.make_async_copy(hx_ref, pool.at[0, :, pl.ds(LOC, own)], own_sem.at[2]),
        pltpu.make_async_copy(
            state_ref.at[:, pl.ds(pl.multiple_of(me * LOC, LOC), LOC)],
            recv.at[member_rows(me), :], own_sem.at[3]),
        pltpu.make_async_copy(value_ref, pairs.at[0, 1], own_sem.at[4]),
        pltpu.make_async_copy(rinv_ref, pairs.at[1, 1], own_sem.at[5]),
    ]
    for copy in local:
        copy.start()
    pl.semaphore_wait(barrier, 4)

    def hop_copy(h, way, c):
        source = hx_ref if h == 1 else pool.at[2 * h - 3 + way]
        start = c * cut_width
        return pltpu.make_async_remote_copy(
            src_ref=source.at[:, pl.ds(start + (0 if h == 1 else LOC), cut_width)],
            dst_ref=pool.at[2 * h - 1 + way, :, pl.ds(LOC + start, cut_width)],
            send_sem=hop_send.at[h - 1, way, c], recv_sem=hop_recv.at[h - 1, way, c],
            device_id={"member": peer(1 - 2 * way)}, device_id_type=MESH,
        )

    def halo_copy(slot, side):
        source = hx_ref if slot == 0 else pool.at[slot]
        start = (0 if slot == 0 else LOC) + (0 if side else own - LOC)
        return pltpu.make_async_remote_copy(
            src_ref=source.at[:, pl.ds(start, LOC)],
            dst_ref=pool.at[slot, :, pl.ds(LOC + own if side else 0, LOC)],
            send_sem=halo_send.at[slot, side], recv_sem=halo_recv.at[slot, side],
            device_id={"tile": prv if side else nxt}, device_id_type=MESH,
        )

    def pair_copy(which, side):
        return pltpu.make_async_remote_copy(
            src_ref=rinv_ref if which else value_ref,
            dst_ref=pairs.at[which, 2 if side else 0],
            send_sem=pair_send.at[which, side], recv_sem=pair_recv.at[which, side],
            device_id={"tile": prv if side else nxt}, device_id_type=MESH,
        )

    def far_copy(way, j):
        target = peer(j if way == 0 else -j)
        source_rows = member_rows(peer(-NEAR if way == 0 else NEAR))
        lanes = pl.ds(0, LOC)
        if j == n // 2 - NEAR:
            lanes = pl.ds(way * (LOC // 2), LOC // 2)
        return pltpu.make_async_remote_copy(
            src_ref=stage.at[way, j - 1, :, lanes],
            dst_ref=obs.at[source_rows, lanes],
            send_sem=far_send.at[way, j - 1], recv_sem=far_recv.at[way, j - 1],
            device_id={"member": target}, device_id_type=MESH,
        )

    def in_copy(d, c):
        t = peer(d)
        return pltpu.make_async_remote_copy(
            src_ref=state_ref.at[:, pl.ds(pl.multiple_of(t * LOC + c * width, LANES), width)],
            dst_ref=recv.at[member_rows(me), pl.ds(c * width, width)],
            send_sem=in_send.at[c, d], recv_sem=in_recv.at[c, d],
            device_id={"member": t}, device_id_type=MESH,
        )

    def back_copy(d, c):
        t = peer(d)
        return pltpu.make_async_remote_copy(
            src_ref=result.at[member_rows(t), pl.ds(c * width, width)],
            dst_ref=out_ref.at[:, pl.ds(pl.multiple_of(me * LOC + c * width, LANES), width)],
            send_sem=back_send.at[c, d], recv_sem=back_recv.at[c, d],
            device_id={"member": t}, device_id_type=MESH,
        )

    def fill(place):
        for c, d in FILL[place]:
            for distance in sorted({d, n - d}):
                in_copy(distance, c).start()

    for c in range(CUTS):
        for way in range(2):
            hop_copy(1, way, c).start()
    for side in range(2):
        for which in range(2):
            pair_copy(which, side).start()
        halo_copy(0, side).start()

    known, stage_no = 1, 0
    while known < n // 2:
        greet(reach_sem.at[stage_no], "member", (peer(known), peer(-known)))
        pl.semaphore_wait(reach_sem.at[stage_no], 2)
        known, stage_no = (2 * known if stage_no else 2), stage_no + 1

    for copy in local:
        copy.wait()

    def pick(source, height, patch, puts):
        row = index_ref[pl.ds(patch, 1), :]
        last = total // LANES - WINDOW
        first = jnp.minimum(jnp.min(row, axis=1, keepdims=True) >> 7, last)
        offset = row - first * LANES
        group, lane = offset >> 7, offset & (LANES - 1)
        shape = (8, LANES)
        steps = [bit for bit in (32, 16, 8, 4, 2, 1) if bit <= last]
        chosen = [jnp.broadcast_to(first & bit, shape) != 0 for bit in steps]

        def body(r, carry):
            line = pl.ds(pl.multiple_of(r * 8, 8), 8)
            found = [source[line, h * LANES:(h + 1) * LANES] for h in range(total // LANES)]
            for bit, mask in zip(steps, chosen):
                found = [jnp.where(mask, found[i + bit], found[i])
                         for i in range(min(WINDOW + bit - 1, len(found) - bit))]
            for g in range(LOC // LANES):
                cut = slice(g * LANES, (g + 1) * LANES)
                lane_b = jnp.broadcast_to(lane[:, cut], shape)
                group_b = jnp.broadcast_to(group[:, cut], shape)
                value = jnp.take_along_axis(found[0], lane_b, axis=1)
                for h in range(1, WINDOW):
                    moved = jnp.take_along_axis(found[h], lane_b, axis=1)
                    value = jnp.where(group_b == h, moved, value)
                puts[line, cut] = value
            return carry

        lax.fori_loop(0, height // 8, body, 0)

    def widen(slot):
        wide[...] = pool[slot].astype(F32)

    def near_pick(slot, m):
        for side in range(2):
            halo_copy(slot, side).wait_recv()
        widen(slot)
        pick(wide, rows, me, picked)
        obs[member_rows(m), :] = picked[...].astype(BF16)

    fill(0)
    for h in range(1, NEAR + 1):
        for c in range(CUTS):
            for way in range(2):
                hop_copy(h, way, c).wait_recv()
                if h < NEAR:
                    hop_copy(h + 1, way, c).start()
        for way in range(2):
            for side in range(2):
                halo_copy(2 * h - 1 + way, side).start()
        fill(h)
        if h == 1:
            near_pick(0, me)
        if h > 1:
            for way in range(2):
                near_pick(2 * h - 3 + way, peer((h - 1) * (2 * way - 1)))
    for way in range(2):
        slot = 2 * NEAR - 1 + way
        for side in range(2):
            halo_copy(slot, side).wait_recv()
        widen(slot)
        for j in range(n // 2 - NEAR, 0, -1):
            pick(wide, rows, peer(j if way == 0 else -j), picked)
            stage[way, j - 1] = picked[...].astype(BF16)
            far_copy(way, j).start()
    fill(NEAR + 1)
    for way in range(2):
        widen(2 * NEAR - 1 + way)
        pick(wide, rows, me, picked)
        obs[member_rows(peer(NEAR * (2 * way - 1))), :] = picked[...].astype(BF16)

    pair_wide[...] = jnp.zeros_like(pair_wide)
    for which in range(2):
        for side in range(2):
            pair_copy(which, side).wait_recv()
        lines = [pairs[which, place].astype(F32) for place in range(3)]
        edge = LOC // LANES
        lines = jnp.concatenate([lines[0][own // LANES - edge:], lines[1], lines[2][:edge]], axis=0)
        for h in range(total // LANES):
            pair_wide[which:which + 1, h * LANES:(h + 1) * LANES] = lines[h:h + 1, :]
    pick(pair_wide, 8, me, picked)
    value_row, rinv_row = picked[0:1, :], picked[1:2, :]
    root = jnp.sqrt(rinv_row * weight_ref[...])

    for way in range(2):
        for j in range(n // 2 - NEAR, 0, -1):
            far_copy(way, j).wait()

    parts = []
    step = 256
    for s in range(0, LOC, step):
        cut = slice(s, s + step)
        block = obs[:, cut].astype(F32)
        mean = jnp.sum(block, axis=0, keepdims=True) * (1.0 / members)
        scaled[:, cut] = ((block - mean) * root[:, cut]).astype(BF16)
        parts.append((value_row[:, cut] - mean) * root[:, cut])
    innovation = jnp.concatenate(parts, axis=1)
    high = innovation.astype(BF16).astype(F32)
    mid = (innovation - high).astype(BF16).astype(F32)
    low = innovation - high - mid
    split = jnp.concatenate([high, mid, low, jnp.zeros((13, LOC), F32)], axis=0).astype(BF16)
    projection = jnp.sum(mm(split, scaled[...], ((1,), (1,))), axis=0, keepdims=True)

    def eye(r):
        shape = (ROWS, members)
        return (lax.broadcasted_iota(jnp.int32, shape, 0) + r
                == lax.broadcasted_iota(jnp.int32, shape, 1))

    pieces = range(0, members, ROWS)
    square = jnp.zeros((1, members), F32)
    for r in pieces:
        gram = mm(scaled[r:r + ROWS, :], scaled[...], ((1,), (1,)))
        piece = jnp.where(eye(r), gram + (members - 1.0), gram)
        system[r:r + ROWS, :] = piece
        square = square + jnp.sum(piece * piece, axis=0, keepdims=True)
    norm = jnp.sqrt(jnp.sum(square, axis=1, keepdims=True))

    def half_of(product, r):
        scaled_product = -0.5 * product
        return jnp.where(eye(r), 1.5 + scaled_product, scaled_product).astype(BF16)

    for r in pieces:
        first = (system[r:r + ROWS, :] / norm).astype(BF16)
        upper[0, r:r + ROWS, :] = first
        lower[0, r:r + ROWS, :] = half_of(first.astype(F32), r)
    for r in pieces:
        upper[1, r:r + ROWS, :] = mm(upper[0, r:r + ROWS, :], lower[0]).astype(BF16)
    for sweep in range(1, NS_ITERS):
        up, new_up = sweep % 2, (sweep + 1) % 2
        low_now, low_new = (sweep - 1) % 2, sweep % 2
        for r in pieces:
            half[r:r + ROWS, :] = half_of(mm(lower[low_now, r:r + ROWS, :], upper[up]), r)
        if sweep + 1 < NS_ITERS:
            for r in pieces:
                upper[new_up, r:r + ROWS, :] = mm(upper[up, r:r + ROWS, :], half[...]).astype(BF16)
            for r in pieces:
                lower[low_new, r:r + ROWS, :] = mm(half[r:r + ROWS, :], lower[low_now]).astype(BF16)
        else:
            for r in pieces:
                system[r:r + ROWS, :] = mm(half[r:r + ROWS, :], lower[low_now]) / jnp.sqrt(norm)
    invroot = system
    highest = lax.Precision.HIGHEST
    vector = jnp.broadcast_to(projection, (8, members))
    for _ in range(2):
        vector = mm(vector, invroot[...], ((1,), (1,)), highest)
    mean_w = vector[0:1]
    scale = (members - 1.0) ** 0.5
    for r in pieces:
        trans[r:r + ROWS, :] = (scale * invroot[:, r:r + ROWS].T + mean_w).astype(BF16)

    own_back = []
    for c in range(CHUNKS):
        def wait_in(d, carry):
            in_copy(d, c).wait()
            return carry

        lax.fori_loop(1, n, wait_in, 0)
        cut = slice(c * width, (c + 1) * width)
        block = recv[:, cut].astype(F32)
        mean = jnp.sum(block, axis=0, keepdims=True) * (1.0 / members)
        pert[...] = (block - mean).astype(BF16)
        for r in pieces:
            result[r:r + ROWS, cut] = (mean + mm(trans[r:r + ROWS, :], pert[...])).astype(BF16)

        def start_back(k, carry):
            back_copy(nth(k), c).start()
            return carry

        lax.fori_loop(0, n - 1, start_back, 0)
        copy = pltpu.make_async_copy(
            result.at[member_rows(me), pl.ds(c * width, width)],
            out_ref.at[:, pl.ds(pl.multiple_of(me * LOC + c * width, LANES), width)],
            own_sem.at[6 + c],
        )
        copy.start()
        own_back.append(copy)
    for c in range(CHUNKS):
        def wait_back(d, carry):
            back_copy(d, c).wait()
            return carry

        lax.fori_loop(1, n, wait_back, 0)
        own_back[c].wait()
    for side in range(2):
        for which in range(2):
            pair_copy(which, side).wait_send()
        for slot in range(2 * NEAR + 1):
            halo_copy(slot, side).wait_send()
    for h in range(1, NEAR + 1):
        for way in range(2):
            for c in range(CUTS):
                hop_copy(h, way, c).wait_send()


def on_device(n, tiles, hx, obs_value, obs_rinv, obs_index, loc_weight, state):
    rows, own = hx.shape
    members = rows * n
    value, rinv = obs_value.reshape(own // LANES, LANES), obs_rinv.reshape(own // LANES, LANES)
    hbm = pl.BlockSpec(memory_space=pltpu.HBM)
    dma = pltpu.SemaphoreType.DMA
    total = own + 2 * LOC
    return pl.pallas_call(
        functools.partial(kernel, n, tiles),
        out_shape=jax.ShapeDtypeStruct(state.shape, BF16),
        in_specs=[hbm] * 6,
        out_specs=pl.BlockSpec(memory_space=pltpu.VMEM),
        scratch_shapes=[
            pltpu.VMEM((2 * NEAR + 1, rows, total), BF16),
            pltpu.VMEM((rows, total), F32),
            pltpu.VMEM((2, 3, own // LANES, LANES), BF16),
            pltpu.VMEM((8, total), F32),
            pltpu.VMEM((n, LOC), jnp.int32),
            pltpu.VMEM((1, LOC), F32),
            pltpu.VMEM((rows, LOC), F32),
            pltpu.VMEM((2, n // 2 - NEAR, rows, LOC), BF16),
            pltpu.VMEM((members, LOC), BF16),
            pltpu.VMEM((members, LOC), BF16),
            pltpu.VMEM((members, LOC), BF16),
            pltpu.VMEM((members, members), F32),
            pltpu.VMEM((2, members, members), BF16),
            pltpu.VMEM((2, members, members), BF16),
            pltpu.VMEM((members, members), BF16),
            pltpu.VMEM((members, members), BF16),
            pltpu.VMEM((members, LOC // CHUNKS), BF16),
            pltpu.VMEM((members, LOC), BF16),
            dma((NEAR, 2, CUTS)), dma((NEAR, 2, CUTS)),
            dma((2 * NEAR + 1, 2)), dma((2 * NEAR + 1, 2)), dma((2, 2)), dma((2, 2)),
            dma((2, n // 2 - NEAR)), dma((2, n // 2 - NEAR)),
            dma((CHUNKS, n)), dma((CHUNKS, n)), dma((CHUNKS, n)), dma((CHUNKS, n)),
            dma((6 + CHUNKS,)), pltpu.SemaphoreType.REGULAR((4,)),
        ],
        compiler_params=pltpu.CompilerParams(
            collective_id=0, has_side_effects=True, vmem_limit_bytes=40 << 20
        ),
        cost_estimate=pl.CostEstimate(
            flops=3 * 10**9, bytes_accessed=4 * 2**20, transcendentals=0),
    )(*(pltpu.with_memory_space_constraint(x, pltpu.HBM)
        for x in (hx, value, rinv, obs_index, loc_weight, state)))


def solution(mesh):
    in_specs = (
        P("member", "tile"),
        P("tile"),
        P("tile"),
        P("tile", None),
        P(("tile", "member"), None),
        P("member", "tile"),
    )
    return jax.shard_map(
        functools.partial(on_device, mesh.shape["member"], mesh.shape["tile"]),
        mesh=mesh, in_specs=in_specs, out_specs=P("member", "tile"), check_vma=False,
    )
```

```python
import functools

import jax
import jax.numpy as jnp
from jax import lax
from jax.experimental import pallas as pl
from jax.experimental.pallas import tpu as pltpu
from jax.sharding import PartitionSpec as P

MESH = pl.DeviceIdType.MESH
F32, BF16 = jnp.float32, jnp.bfloat16
LOC = 1024
NS_ITERS = 3
LANES = 128
ROWS = 128
WINDOW = 17
CHUNKS = 2
FILL = (
    ((0, 2), (0, 3)),
    ((0, 5),),
    ((0, 4), (0, 1)),
    ((0, 6),),
    ((0, 7), (0, 8), (1, 6), (1, 4)),
    ((1, 8), (1, 7), (1, 5), (1, 3), (1, 2), (1, 1)),
)
NEAR = 4
CUTS = 2


def mm(left, right, dims=((1,), (0,)), precision=None):
    return lax.dot_general(
        left, right, (dims, ((), ())), precision=precision, preferred_element_type=F32
    )


def kernel(
    n, tiles,
    hx_ref, value_ref, rinv_ref, index_hbm, weight_hbm, state_ref,
    out_ref,
    pool, wide, pairs, pair_wide, index_ref, weight_ref, picked, stage, obs, recv, scaled, system,
    upper, lower, half, trans, pert, result,
    hop_send, hop_recv, halo_send, halo_recv, pair_send, pair_recv, far_send, far_recv,
    in_send, in_recv, back_send, back_recv, own_sem, reach_sem,
):
    me = lax.axis_index("member")
    tile = lax.axis_index("tile")
    nxt, prv = lax.rem(tile + 1, tiles), lax.rem(tile + tiles - 1, tiles)
    rows, own = hx_ref.shape
    members = rows * n
    total = own + 2 * LOC
    width = LOC // CHUNKS
    cut_width = own // CUTS

    def peer(d):
        return lax.rem(me + d + n, n)

    def member_rows(m):
        return pl.ds(pl.multiple_of(m * rows, rows), rows)

    def nth(k):
        step = n // 2 - (k + 1) // 2
        return jnp.where(k % 2 == 1, step, n - step)

    def greet(semaphore, axis, others):
        for other in others:
            pl.semaphore_signal(semaphore, inc=1, device_id={axis: other}, device_id_type=MESH)

    barrier = pltpu.get_barrier_semaphore()
    greet(barrier, "member", (peer(1), peer(-1)))
    greet(barrier, "tile", (nxt, prv))
    local = [
        pltpu.make_async_copy(index_hbm, index_ref, own_sem.at[0]),
        pltpu.make_async_copy(weight_hbm, weight_ref, own_sem.at[1]),
        pltpu.make_async_copy(hx_ref, pool.at[0, :, pl.ds(LOC, own)], own_sem.at[2]),
        pltpu.make_async_copy(
            state_ref.at[:, pl.ds(pl.multiple_of(me * LOC, LOC), LOC)],
            recv.at[member_rows(me), :], own_sem.at[3]),
        pltpu.make_async_copy(value_ref, pairs.at[0, 1], own_sem.at[4]),
        pltpu.make_async_copy(rinv_ref, pairs.at[1, 1], own_sem.at[5]),
    ]
    for copy in local:
        copy.start()
    pl.semaphore_wait(barrier, 4)

    def hop_copy(h, way, c):
        source = hx_ref if h == 1 else pool.at[2 * h - 3 + way]
        start = c * cut_width
        return pltpu.make_async_remote_copy(
            src_ref=source.at[:, pl.ds(start + (0 if h == 1 else LOC), cut_width)],
            dst_ref=pool.at[2 * h - 1 + way, :, pl.ds(LOC + start, cut_width)],
            send_sem=hop_send.at[h - 1, way, c], recv_sem=hop_recv.at[h - 1, way, c],
            device_id={"member": peer(1 - 2 * way)}, device_id_type=MESH,
        )

    def halo_copy(slot, side):
        source = hx_ref if slot == 0 else pool.at[slot]
        start = (0 if slot == 0 else LOC) + (0 if side else own - LOC)
        return pltpu.make_async_remote_copy(
            src_ref=source.at[:, pl.ds(start, LOC)],
            dst_ref=pool.at[slot, :, pl.ds(LOC + own if side else 0, LOC)],
            send_sem=halo_send.at[slot, side], recv_sem=halo_recv.at[slot, side],
            device_id={"tile": prv if side else nxt}, device_id_type=MESH,
        )

    def pair_copy(which, side):
        return pltpu.make_async_remote_copy(
            src_ref=rinv_ref if which else value_ref,
            dst_ref=pairs.at[which, 2 if side else 0],
            send_sem=pair_send.at[which, side], recv_sem=pair_recv.at[which, side],
            device_id={"tile": prv if side else nxt}, device_id_type=MESH,
        )

    def far_copy(way, j):
        target = peer(j if way == 0 else -j)
        source_rows = member_rows(peer(-NEAR if way == 0 else NEAR))
        lanes = pl.ds(0, LOC)
        if j == n // 2 - NEAR:
            lanes = pl.ds(way * (LOC // 2), LOC // 2)
        return pltpu.make_async_remote_copy(
            src_ref=stage.at[way, j - 1, :, lanes],
            dst_ref=obs.at[source_rows, lanes],
            send_sem=far_send.at[way, j - 1], recv_sem=far_recv.at[way, j - 1],
            device_id={"member": target}, device_id_type=MESH,
        )

    def in_copy(d, c):
        t = peer(d)
        return pltpu.make_async_remote_copy(
            src_ref=state_ref.at[:, pl.ds(pl.multiple_of(t * LOC + c * width, LANES), width)],
            dst_ref=recv.at[member_rows(me), pl.ds(c * width, width)],
            send_sem=in_send.at[c, d], recv_sem=in_recv.at[c, d],
            device_id={"member": t}, device_id_type=MESH,
        )

    def back_copy(d, c):
        t = peer(d)
        return pltpu.make_async_remote_copy(
            src_ref=result.at[member_rows(t), pl.ds(c * width, width)],
            dst_ref=out_ref.at[:, pl.ds(pl.multiple_of(me * LOC + c * width, LANES), width)],
            send_sem=back_send.at[c, d], recv_sem=back_recv.at[c, d],
            device_id={"member": t}, device_id_type=MESH,
        )

    def fill(place):
        for c, d in FILL[place]:
            for distance in sorted({d, n - d}):
                in_copy(distance, c).start()

    for c in range(CUTS):
        for way in range(2):
            hop_copy(1, way, c).start()
    for side in range(2):
        for which in range(2):
            pair_copy(which, side).start()
        halo_copy(0, side).start()

    known, stage_no = 1, 0
    while known < n // 2:
        greet(reach_sem.at[stage_no], "member", (peer(known), peer(-known)))
        pl.semaphore_wait(reach_sem.at[stage_no], 2)
        known, stage_no = (2 * known if stage_no else 2), stage_no + 1

    for copy in local:
        copy.wait()

    def pick(source, height, patch, puts):
        row = index_ref[pl.ds(patch, 1), :]
        last = total // LANES - WINDOW
        first = jnp.minimum(jnp.min(row, axis=1, keepdims=True) >> 7, last)
        offset = row - first * LANES
        group, lane = offset >> 7, offset & (LANES - 1)
        shape = (8, LANES)
        steps = [bit for bit in (32, 16, 8, 4, 2, 1) if bit <= last]
        chosen = [jnp.broadcast_to(first & bit, shape) != 0 for bit in steps]

        def body(r, carry):
            line = pl.ds(pl.multiple_of(r * 8, 8), 8)
            found = [source[line, h * LANES:(h + 1) * LANES] for h in range(total // LANES)]
            for bit, mask in zip(steps, chosen):
                found = [jnp.where(mask, found[i + bit], found[i])
                         for i in range(min(WINDOW + bit - 1, len(found) - bit))]
            for g in range(LOC // LANES):
                cut = slice(g * LANES, (g + 1) * LANES)
                lane_b = jnp.broadcast_to(lane[:, cut], shape)
                group_b = jnp.broadcast_to(group[:, cut], shape)
                value = jnp.take_along_axis(found[0], lane_b, axis=1)
                for h in range(1, WINDOW):
                    moved = jnp.take_along_axis(found[h], lane_b, axis=1)
                    value = jnp.where(group_b == h, moved, value)
                puts[line, cut] = value
            return carry

        lax.fori_loop(0, height // 8, body, 0)

    def widen(slot, way=0):
        wide[way] = pool[slot].astype(F32)

    def near_pick(slot, m):
        for side in range(2):
            halo_copy(slot, side).wait_recv()
        widen(slot)
        pick(wide.at[0], rows, me, picked)
        obs[member_rows(m), :] = picked[...].astype(BF16)

    fill(0)
    for h in range(1, NEAR + 1):
        for c in range(CUTS):
            for way in range(2):
                hop_copy(h, way, c).wait_recv()
                if h < NEAR:
                    hop_copy(h + 1, way, c).start()
        for way in range(2):
            for side in range(2):
                halo_copy(2 * h - 1 + way, side).start()
        fill(h)
        if h == 1:
            near_pick(0, me)
        if h > 1:
            for way in range(2):
                near_pick(2 * h - 3 + way, peer((h - 1) * (2 * way - 1)))
    for way in range(2):
        slot = 2 * NEAR - 1 + way
        for side in range(2):
            halo_copy(slot, side).wait_recv()
        widen(slot, way)
    for j in range(n // 2 - NEAR, 0, -1):
        for way in range(2):
            pick(wide.at[way], rows, peer(j if way == 0 else -j), picked)
            stage[way, j - 1] = picked[...].astype(BF16)
            far_copy(way, j).start()
    fill(NEAR + 1)
    for way in range(2):
        pick(wide.at[way], rows, me, picked)
        obs[member_rows(peer(NEAR * (2 * way - 1))), :] = picked[...].astype(BF16)

    pair_wide[...] = jnp.zeros_like(pair_wide)
    for which in range(2):
        for side in range(2):
            pair_copy(which, side).wait_recv()
        lines = [pairs[which, place].astype(F32) for place in range(3)]
        edge = LOC // LANES
        lines = jnp.concatenate([lines[0][own // LANES - edge:], lines[1], lines[2][:edge]], axis=0)
        for h in range(total // LANES):
            pair_wide[which:which + 1, h * LANES:(h + 1) * LANES] = lines[h:h + 1, :]
    pick(pair_wide, 8, me, picked)
    value_row, rinv_row = picked[0:1, :], picked[1:2, :]
    root = jnp.sqrt(rinv_row * weight_ref[...])

    for way in range(2):
        for j in range(n // 2 - NEAR, 0, -1):
            far_copy(way, j).wait()

    parts = []
    step = 256
    for s in range(0, LOC, step):
        cut = slice(s, s + step)
        block = obs[:, cut].astype(F32)
        mean = jnp.sum(block, axis=0, keepdims=True) * (1.0 / members)
        scaled[:, cut] = ((block - mean) * root[:, cut]).astype(BF16)
        parts.append((value_row[:, cut] - mean) * root[:, cut])
    innovation = jnp.concatenate(parts, axis=1)
    high = innovation.astype(BF16).astype(F32)
    mid = (innovation - high).astype(BF16).astype(F32)
    low = innovation - high - mid
    split = jnp.concatenate([high, mid, low, jnp.zeros((13, LOC), F32)], axis=0).astype(BF16)
    projection = jnp.sum(mm(split, scaled[...], ((1,), (1,))), axis=0, keepdims=True)

    def eye(r):
        shape = (ROWS, members)
        return (lax.broadcasted_iota(jnp.int32, shape, 0) + r
                == lax.broadcasted_iota(jnp.int32, shape, 1))

    pieces = range(0, members, ROWS)
    square = jnp.zeros((1, members), F32)
    for r in pieces:
        gram = mm(scaled[r:r + ROWS, :], scaled[...], ((1,), (1,)))
        piece = jnp.where(eye(r), gram + (members - 1.0), gram)
        system[r:r + ROWS, :] = piece
        square = square + jnp.sum(piece * piece, axis=0, keepdims=True)
    norm = jnp.sqrt(jnp.sum(square, axis=1, keepdims=True))

    def half_of(product, r):
        scaled_product = -0.5 * product
        return jnp.where(eye(r), 1.5 + scaled_product, scaled_product).astype(BF16)

    for r in pieces:
        first = (system[r:r + ROWS, :] / norm).astype(BF16)
        upper[0, r:r + ROWS, :] = first
        lower[0, r:r + ROWS, :] = half_of(first.astype(F32), r)
    for r in pieces:
        upper[1, r:r + ROWS, :] = mm(upper[0, r:r + ROWS, :], lower[0]).astype(BF16)
    for sweep in range(1, NS_ITERS):
        up, new_up = sweep % 2, (sweep + 1) % 2
        low_now, low_new = (sweep - 1) % 2, sweep % 2
        for r in pieces:
            half[r:r + ROWS, :] = half_of(mm(lower[low_now, r:r + ROWS, :], upper[up]), r)
        if sweep + 1 < NS_ITERS:
            for r in pieces:
                upper[new_up, r:r + ROWS, :] = mm(upper[up, r:r + ROWS, :], half[...]).astype(BF16)
            for r in pieces:
                lower[low_new, r:r + ROWS, :] = mm(half[r:r + ROWS, :], lower[low_now]).astype(BF16)
        else:
            for r in pieces:
                system[r:r + ROWS, :] = mm(half[r:r + ROWS, :], lower[low_now]) / jnp.sqrt(norm)
    invroot = system
    highest = lax.Precision.HIGHEST
    vector = jnp.broadcast_to(projection, (8, members))
    for _ in range(2):
        vector = mm(vector, invroot[...], ((1,), (1,)), highest)
    mean_w = vector[0:1]
    scale = (members - 1.0) ** 0.5
    for r in pieces:
        trans[r:r + ROWS, :] = (scale * invroot[:, r:r + ROWS].T + mean_w).astype(BF16)

    own_back = []
    for c in range(CHUNKS):
        def wait_in(d, carry):
            in_copy(d, c).wait()
            return carry

        lax.fori_loop(1, n, wait_in, 0)
        cut = slice(c * width, (c + 1) * width)
        block = recv[:, cut].astype(F32)
        mean = jnp.sum(block, axis=0, keepdims=True) * (1.0 / members)
        pert[...] = (block - mean).astype(BF16)
        for r in pieces:
            result[r:r + ROWS, cut] = (mean + mm(trans[r:r + ROWS, :], pert[...])).astype(BF16)

        def start_back(k, carry):
            back_copy(nth(k), c).start()
            return carry

        lax.fori_loop(0, n - 1, start_back, 0)
        copy = pltpu.make_async_copy(
            result.at[member_rows(me), pl.ds(c * width, width)],
            out_ref.at[:, pl.ds(pl.multiple_of(me * LOC + c * width, LANES), width)],
            own_sem.at[6 + c],
        )
        copy.start()
        own_back.append(copy)
    for c in range(CHUNKS):
        def wait_back(d, carry):
            back_copy(d, c).wait()
            return carry

        lax.fori_loop(1, n, wait_back, 0)
        own_back[c].wait()
    for side in range(2):
        for which in range(2):
            pair_copy(which, side).wait_send()
        for slot in range(2 * NEAR + 1):
            halo_copy(slot, side).wait_send()
    for h in range(1, NEAR + 1):
        for way in range(2):
            for c in range(CUTS):
                hop_copy(h, way, c).wait_send()


def on_device(n, tiles, hx, obs_value, obs_rinv, obs_index, loc_weight, state):
    rows, own = hx.shape
    members = rows * n
    value, rinv = obs_value.reshape(own // LANES, LANES), obs_rinv.reshape(own // LANES, LANES)
    hbm = pl.BlockSpec(memory_space=pltpu.HBM)
    dma = pltpu.SemaphoreType.DMA
    total = own + 2 * LOC
    return pl.pallas_call(
        functools.partial(kernel, n, tiles),
        out_shape=jax.ShapeDtypeStruct(state.shape, BF16),
        in_specs=[hbm] * 6,
        out_specs=pl.BlockSpec(memory_space=pltpu.VMEM),
        scratch_shapes=[
            pltpu.VMEM((2 * NEAR + 1, rows, total), BF16),
            pltpu.VMEM((2, rows, total), F32),
            pltpu.VMEM((2, 3, own // LANES, LANES), BF16),
            pltpu.VMEM((8, total), F32),
            pltpu.VMEM((n, LOC), jnp.int32),
            pltpu.VMEM((1, LOC), F32),
            pltpu.VMEM((rows, LOC), F32),
            pltpu.VMEM((2, n // 2 - NEAR, rows, LOC), BF16),
            pltpu.VMEM((members, LOC), BF16),
            pltpu.VMEM((members, LOC), BF16),
            pltpu.VMEM((members, LOC), BF16),
            pltpu.VMEM((members, members), F32),
            pltpu.VMEM((2, members, members), BF16),
            pltpu.VMEM((2, members, members), BF16),
            pltpu.VMEM((members, members), BF16),
            pltpu.VMEM((members, members), BF16),
            pltpu.VMEM((members, LOC // CHUNKS), BF16),
            pltpu.VMEM((members, LOC), BF16),
            dma((NEAR, 2, CUTS)), dma((NEAR, 2, CUTS)),
            dma((2 * NEAR + 1, 2)), dma((2 * NEAR + 1, 2)), dma((2, 2)), dma((2, 2)),
            dma((2, n // 2 - NEAR)), dma((2, n // 2 - NEAR)),
            dma((CHUNKS, n)), dma((CHUNKS, n)), dma((CHUNKS, n)), dma((CHUNKS, n)),
            dma((6 + CHUNKS,)), pltpu.SemaphoreType.REGULAR((4,)),
        ],
        compiler_params=pltpu.CompilerParams(
            collective_id=0, has_side_effects=True, vmem_limit_bytes=40 << 20
        ),
        cost_estimate=pl.CostEstimate(
            flops=3 * 10**9, bytes_accessed=4 * 2**20, transcendentals=0),
    )(*(pltpu.with_memory_space_constraint(x, pltpu.HBM)
        for x in (hx, value, rinv, obs_index, loc_weight, state)))


def solution(mesh):
    in_specs = (
        P("member", "tile"),
        P("tile"),
        P("tile"),
        P("tile", None),
        P(("tile", "member"), None),
        P("member", "tile"),
    )
    return jax.shard_map(
        functools.partial(on_device, mesh.shape["member"], mesh.shape["tile"]),
        mesh=mesh, in_specs=in_specs, out_specs=P("member", "tile"), check_vma=False,
    )
```

```python
import functools

import jax
import jax.numpy as jnp
from jax import lax
from jax.experimental import pallas as pl
from jax.experimental.pallas import tpu as pltpu
from jax.sharding import PartitionSpec as P

MESH = pl.DeviceIdType.MESH
F32, BF16 = jnp.float32, jnp.bfloat16
LOC = 1024
NS_ITERS = 3
LANES = 128
ROWS = 128
WINDOW = 17
CHUNKS = 2
FILL = (
    ((0, 2), (0, 3)),
    ((0, 5),),
    ((0, 4), (0, 1)),
    ((0, 6),),
    ((0, 7), (0, 8), (1, 6), (1, 4)),
    ((1, 8), (1, 7), (1, 5), (1, 3), (1, 2), (1, 1)),
)
NEAR = 4
CUTS = 1


def mm(left, right, dims=((1,), (0,)), precision=None):
    return lax.dot_general(
        left, right, (dims, ((), ())), precision=precision, preferred_element_type=F32
    )


def kernel(
    n, tiles,
    hx_ref, value_ref, rinv_ref, index_hbm, weight_hbm, state_ref,
    out_ref,
    pool, wide, pairs, pair_wide, index_ref, weight_ref, picked, stage, obs, recv, scaled, system,
    upper, lower, half, trans, pert, result,
    hop_send, hop_recv, halo_send, halo_recv, pair_send, pair_recv, far_send, far_recv,
    in_send, in_recv, back_send, back_recv, own_sem, reach_sem,
):
    me = lax.axis_index("member")
    tile = lax.axis_index("tile")
    nxt, prv = lax.rem(tile + 1, tiles), lax.rem(tile + tiles - 1, tiles)
    rows, own = hx_ref.shape
    members = rows * n
    total = own + 2 * LOC
    width = LOC // CHUNKS
    cut_width = own // CUTS

    def peer(d):
        return lax.rem(me + d + n, n)

    def member_rows(m):
        return pl.ds(pl.multiple_of(m * rows, rows), rows)

    def nth(k):
        step = n // 2 - (k + 1) // 2
        return jnp.where(k % 2 == 1, step, n - step)

    def greet(semaphore, axis, others):
        for other in others:
            pl.semaphore_signal(semaphore, inc=1, device_id={axis: other}, device_id_type=MESH)

    barrier = pltpu.get_barrier_semaphore()
    greet(barrier, "member", (peer(1), peer(-1)))
    greet(barrier, "tile", (nxt, prv))
    local = [
        pltpu.make_async_copy(index_hbm, index_ref, own_sem.at[0]),
        pltpu.make_async_copy(weight_hbm, weight_ref, own_sem.at[1]),
        pltpu.make_async_copy(hx_ref, pool.at[0, :, pl.ds(LOC, own)], own_sem.at[2]),
        pltpu.make_async_copy(
            state_ref.at[:, pl.ds(pl.multiple_of(me * LOC, LOC), LOC)],
            recv.at[member_rows(me), :], own_sem.at[3]),
        pltpu.make_async_copy(value_ref, pairs.at[0, 1], own_sem.at[4]),
        pltpu.make_async_copy(rinv_ref, pairs.at[1, 1], own_sem.at[5]),
    ]
    for copy in local:
        copy.start()
    pl.semaphore_wait(barrier, 4)

    def hop_copy(h, way, c):
        source = hx_ref if h == 1 else pool.at[2 * h - 3 + way]
        start = c * cut_width
        return pltpu.make_async_remote_copy(
            src_ref=source.at[:, pl.ds(start + (0 if h == 1 else LOC), cut_width)],
            dst_ref=pool.at[2 * h - 1 + way, :, pl.ds(LOC + start, cut_width)],
            send_sem=hop_send.at[h - 1, way, c], recv_sem=hop_recv.at[h - 1, way, c],
            device_id={"member": peer(1 - 2 * way)}, device_id_type=MESH,
        )

    def halo_copy(slot, side):
        source = hx_ref if slot == 0 else pool.at[slot]
        start = (0 if slot == 0 else LOC) + (0 if side else own - LOC)
        return pltpu.make_async_remote_copy(
            src_ref=source.at[:, pl.ds(start, LOC)],
            dst_ref=pool.at[slot, :, pl.ds(LOC + own if side else 0, LOC)],
            send_sem=halo_send.at[slot, side], recv_sem=halo_recv.at[slot, side],
            device_id={"tile": prv if side else nxt}, device_id_type=MESH,
        )

    def pair_copy(which, side):
        return pltpu.make_async_remote_copy(
            src_ref=rinv_ref if which else value_ref,
            dst_ref=pairs.at[which, 2 if side else 0],
            send_sem=pair_send.at[which, side], recv_sem=pair_recv.at[which, side],
            device_id={"tile": prv if side else nxt}, device_id_type=MESH,
        )

    def far_copy(way, j):
        target = peer(j if way == 0 else -j)
        source_rows = member_rows(peer(-NEAR if way == 0 else NEAR))
        lanes = pl.ds(0, LOC)
        if j == n // 2 - NEAR:
            lanes = pl.ds(way * (LOC // 2), LOC // 2)
        return pltpu.make_async_remote_copy(
            src_ref=stage.at[way, j - 1, :, lanes],
            dst_ref=obs.at[source_rows, lanes],
            send_sem=far_send.at[way, j - 1], recv_sem=far_recv.at[way, j - 1],
            device_id={"member": target}, device_id_type=MESH,
        )

    def in_copy(d, c):
        t = peer(d)
        return pltpu.make_async_remote_copy(
            src_ref=state_ref.at[:, pl.ds(pl.multiple_of(t * LOC + c * width, LANES), width)],
            dst_ref=recv.at[member_rows(me), pl.ds(c * width, width)],
            send_sem=in_send.at[c, d], recv_sem=in_recv.at[c, d],
            device_id={"member": t}, device_id_type=MESH,
        )

    def back_copy(d, c):
        t = peer(d)
        return pltpu.make_async_remote_copy(
            src_ref=result.at[member_rows(t), pl.ds(c * width, width)],
            dst_ref=out_ref.at[:, pl.ds(pl.multiple_of(me * LOC + c * width, LANES), width)],
            send_sem=back_send.at[c, d], recv_sem=back_recv.at[c, d],
            device_id={"member": t}, device_id_type=MESH,
        )

    def fill(place):
        for c, d in FILL[place]:
            for distance in sorted({d, n - d}):
                in_copy(distance, c).start()

    for c in range(CUTS):
        for way in range(2):
            hop_copy(1, way, c).start()
    for side in range(2):
        for which in range(2):
            pair_copy(which, side).start()
        halo_copy(0, side).start()

    known, stage_no = 1, 0
    while known < n // 2:
        greet(reach_sem.at[stage_no], "member", (peer(known), peer(-known)))
        pl.semaphore_wait(reach_sem.at[stage_no], 2)
        known, stage_no = (2 * known if stage_no else 2), stage_no + 1

    for copy in local:
        copy.wait()

    def pick(source, height, patch, puts):
        row = index_ref[pl.ds(patch, 1), :]
        last = total // LANES - WINDOW
        first = jnp.minimum(jnp.min(row, axis=1, keepdims=True) >> 7, last)
        offset = row - first * LANES
        group, lane = offset >> 7, offset & (LANES - 1)
        shape = (8, LANES)
        steps = [bit for bit in (32, 16, 8, 4, 2, 1) if bit <= last]
        chosen = [jnp.broadcast_to(first & bit, shape) != 0 for bit in steps]

        def body(r, carry):
            line = pl.ds(pl.multiple_of(r * 8, 8), 8)
            found = [source[line, h * LANES:(h + 1) * LANES] for h in range(total // LANES)]
            for bit, mask in zip(steps, chosen):
                found = [jnp.where(mask, found[i + bit], found[i])
                         for i in range(min(WINDOW + bit - 1, len(found) - bit))]
            for g in range(LOC // LANES):
                cut = slice(g * LANES, (g + 1) * LANES)
                lane_b = jnp.broadcast_to(lane[:, cut], shape)
                group_b = jnp.broadcast_to(group[:, cut], shape)
                value = jnp.take_along_axis(found[0], lane_b, axis=1)
                for h in range(1, WINDOW):
                    moved = jnp.take_along_axis(found[h], lane_b, axis=1)
                    value = jnp.where(group_b == h, moved, value)
                puts[line, cut] = value
            return carry

        lax.fori_loop(0, height // 8, body, 0)

    def widen(slot, way=0):
        wide[way] = pool[slot].astype(F32)

    def near_pick(slot, m):
        for side in range(2):
            halo_copy(slot, side).wait_recv()
        widen(slot)
        pick(wide.at[0], rows, me, picked)
        obs[member_rows(m), :] = picked[...].astype(BF16)

    fill(0)
    for h in range(1, NEAR + 1):
        for c in range(CUTS):
            for way in range(2):
                hop_copy(h, way, c).wait_recv()
                if h < NEAR:
                    hop_copy(h + 1, way, c).start()
        for way in range(2):
            for side in range(2):
                halo_copy(2 * h - 1 + way, side).start()
        fill(h)
        if h == 1:
            near_pick(0, me)
        if h > 1:
            for way in range(2):
                near_pick(2 * h - 3 + way, peer((h - 1) * (2 * way - 1)))
    for way in range(2):
        slot = 2 * NEAR - 1 + way
        for side in range(2):
            halo_copy(slot, side).wait_recv()
        widen(slot, way)
    for j in range(n // 2 - NEAR, 0, -1):
        for way in range(2):
            pick(wide.at[way], rows, peer(j if way == 0 else -j), picked)
            stage[way, j - 1] = picked[...].astype(BF16)
            far_copy(way, j).start()
    fill(NEAR + 1)
    for way in range(2):
        pick(wide.at[way], rows, me, picked)
        obs[member_rows(peer(NEAR * (2 * way - 1))), :] = picked[...].astype(BF16)

    pair_wide[...] = jnp.zeros_like(pair_wide)
    for which in range(2):
        for side in range(2):
            pair_copy(which, side).wait_recv()
        lines = [pairs[which, place].astype(F32) for place in range(3)]
        edge = LOC // LANES
        lines = jnp.concatenate([lines[0][own // LANES - edge:], lines[1], lines[2][:edge]], axis=0)
        for h in range(total // LANES):
            pair_wide[which:which + 1, h * LANES:(h + 1) * LANES] = lines[h:h + 1, :]
    pick(pair_wide, 8, me, picked)
    value_row, rinv_row = picked[0:1, :], picked[1:2, :]
    root = jnp.sqrt(rinv_row * weight_ref[...])

    for way in range(2):
        for j in range(n // 2 - NEAR, 0, -1):
            far_copy(way, j).wait()

    parts = []
    step = 256
    for s in range(0, LOC, step):
        cut = slice(s, s + step)
        block = obs[:, cut].astype(F32)
        mean = jnp.sum(block, axis=0, keepdims=True) * (1.0 / members)
        scaled[:, cut] = ((block - mean) * root[:, cut]).astype(BF16)
        parts.append((value_row[:, cut] - mean) * root[:, cut])
    innovation = jnp.concatenate(parts, axis=1)
    high = innovation.astype(BF16).astype(F32)
    mid = (innovation - high).astype(BF16).astype(F32)
    low = innovation - high - mid
    split = jnp.concatenate([high, mid, low, jnp.zeros((13, LOC), F32)], axis=0).astype(BF16)
    projection = jnp.sum(mm(split, scaled[...], ((1,), (1,))), axis=0, keepdims=True)

    def eye(r):
        shape = (ROWS, members)
        return (lax.broadcasted_iota(jnp.int32, shape, 0) + r
                == lax.broadcasted_iota(jnp.int32, shape, 1))

    pieces = range(0, members, ROWS)
    square = jnp.zeros((1, members), F32)
    for r in pieces:
        gram = mm(scaled[r:r + ROWS, :], scaled[...], ((1,), (1,)))
        piece = jnp.where(eye(r), gram + (members - 1.0), gram)
        system[r:r + ROWS, :] = piece
        square = square + jnp.sum(piece * piece, axis=0, keepdims=True)
    norm = jnp.sqrt(jnp.sum(square, axis=1, keepdims=True))

    def half_of(product, r):
        scaled_product = -0.5 * product
        return jnp.where(eye(r), 1.5 + scaled_product, scaled_product).astype(BF16)

    for r in pieces:
        first = (system[r:r + ROWS, :] / norm).astype(BF16)
        upper[0, r:r + ROWS, :] = first
        lower[0, r:r + ROWS, :] = half_of(first.astype(F32), r)
    for r in pieces:
        upper[1, r:r + ROWS, :] = mm(upper[0, r:r + ROWS, :], lower[0]).astype(BF16)
    for sweep in range(1, NS_ITERS):
        up, new_up = sweep % 2, (sweep + 1) % 2
        low_now, low_new = (sweep - 1) % 2, sweep % 2
        for r in pieces:
            half[r:r + ROWS, :] = half_of(mm(lower[low_now, r:r + ROWS, :], upper[up]), r)
        if sweep + 1 < NS_ITERS:
            for r in pieces:
                upper[new_up, r:r + ROWS, :] = mm(upper[up, r:r + ROWS, :], half[...]).astype(BF16)
            for r in pieces:
                lower[low_new, r:r + ROWS, :] = mm(half[r:r + ROWS, :], lower[low_now]).astype(BF16)
        else:
            for r in pieces:
                system[r:r + ROWS, :] = mm(half[r:r + ROWS, :], lower[low_now]) / jnp.sqrt(norm)
    invroot = system
    highest = lax.Precision.HIGHEST
    vector = jnp.broadcast_to(projection, (8, members))
    for _ in range(2):
        vector = mm(vector, invroot[...], ((1,), (1,)), highest)
    mean_w = vector[0:1]
    scale = (members - 1.0) ** 0.5
    for r in pieces:
        trans[r:r + ROWS, :] = (scale * invroot[:, r:r + ROWS].T + mean_w).astype(BF16)

    own_back = []
    for c in range(CHUNKS):
        def wait_in(d, carry):
            in_copy(d, c).wait()
            return carry

        lax.fori_loop(1, n, wait_in, 0)
        cut = slice(c * width, (c + 1) * width)
        block = recv[:, cut].astype(F32)
        mean = jnp.sum(block, axis=0, keepdims=True) * (1.0 / members)
        pert[...] = (block - mean).astype(BF16)
        for r in pieces:
            result[r:r + ROWS, cut] = (mean + mm(trans[r:r + ROWS, :], pert[...])).astype(BF16)

        def start_back(k, carry):
            back_copy(nth(k), c).start()
            return carry

        lax.fori_loop(0, n - 1, start_back, 0)
        copy = pltpu.make_async_copy(
            result.at[member_rows(me), pl.ds(c * width, width)],
            out_ref.at[:, pl.ds(pl.multiple_of(me * LOC + c * width, LANES), width)],
            own_sem.at[6 + c],
        )
        copy.start()
        own_back.append(copy)
    for c in range(CHUNKS):
        def wait_back(d, carry):
            back_copy(d, c).wait()
            return carry

        lax.fori_loop(1, n, wait_back, 0)
        own_back[c].wait()
    for side in range(2):
        for which in range(2):
            pair_copy(which, side).wait_send()
        for slot in range(2 * NEAR + 1):
            halo_copy(slot, side).wait_send()
    for h in range(1, NEAR + 1):
        for way in range(2):
            for c in range(CUTS):
                hop_copy(h, way, c).wait_send()


def on_device(n, tiles, hx, obs_value, obs_rinv, obs_index, loc_weight, state):
    rows, own = hx.shape
    members = rows * n
    value, rinv = obs_value.reshape(own // LANES, LANES), obs_rinv.reshape(own // LANES, LANES)
    hbm = pl.BlockSpec(memory_space=pltpu.HBM)
    dma = pltpu.SemaphoreType.DMA
    total = own + 2 * LOC
    return pl.pallas_call(
        functools.partial(kernel, n, tiles),
        out_shape=jax.ShapeDtypeStruct(state.shape, BF16),
        in_specs=[hbm] * 6,
        out_specs=pl.BlockSpec(memory_space=pltpu.VMEM),
        scratch_shapes=[
            pltpu.VMEM((2 * NEAR + 1, rows, total), BF16),
            pltpu.VMEM((2, rows, total), F32),
            pltpu.VMEM((2, 3, own // LANES, LANES), BF16),
            pltpu.VMEM((8, total), F32),
            pltpu.VMEM((n, LOC), jnp.int32),
            pltpu.VMEM((1, LOC), F32),
            pltpu.VMEM((rows, LOC), F32),
            pltpu.VMEM((2, n // 2 - NEAR, rows, LOC), BF16),
            pltpu.VMEM((members, LOC), BF16),
            pltpu.VMEM((members, LOC), BF16),
            pltpu.VMEM((members, LOC), BF16),
            pltpu.VMEM((members, members), F32),
            pltpu.VMEM((2, members, members), BF16),
            pltpu.VMEM((2, members, members), BF16),
            pltpu.VMEM((members, members), BF16),
            pltpu.VMEM((members, members), BF16),
            pltpu.VMEM((members, LOC // CHUNKS), BF16),
            pltpu.VMEM((members, LOC), BF16),
            dma((NEAR, 2, CUTS)), dma((NEAR, 2, CUTS)),
            dma((2 * NEAR + 1, 2)), dma((2 * NEAR + 1, 2)), dma((2, 2)), dma((2, 2)),
            dma((2, n // 2 - NEAR)), dma((2, n // 2 - NEAR)),
            dma((CHUNKS, n)), dma((CHUNKS, n)), dma((CHUNKS, n)), dma((CHUNKS, n)),
            dma((6 + CHUNKS,)), pltpu.SemaphoreType.REGULAR((4,)),
        ],
        compiler_params=pltpu.CompilerParams(
            collective_id=0, has_side_effects=True, vmem_limit_bytes=40 << 20
        ),
        cost_estimate=pl.CostEstimate(
            flops=3 * 10**9, bytes_accessed=4 * 2**20, transcendentals=0),
    )(*(pltpu.with_memory_space_constraint(x, pltpu.HBM)
        for x in (hx, value, rinv, obs_index, loc_weight, state)))


def solution(mesh):
    in_specs = (
        P("member", "tile"),
        P("tile"),
        P("tile"),
        P("tile", None),
        P(("tile", "member"), None),
        P("member", "tile"),
    )
    return jax.shard_map(
        functools.partial(on_device, mesh.shape["member"], mesh.shape["tile"]),
        mesh=mesh, in_specs=in_specs, out_specs=P("member", "tile"), check_vma=False,
    )
```
